128 devices in a mesh: ex: 16 (over x, z), tp: 8 (over y, core).
Axes of the slice: x: 4, y: 4, z: 4, core: 2. Of those that a mesh axis runs over, the one named last changes fastest.
Arguments:
- activations: bfloat16 [64, 128, 8192], P('ex', None, 'tp'), may hold values from -6 to 6
- out_grads: bfloat16 [64, 128, 8192], P('ex', None, 'tp'), may hold values from -0.5390625 to 0.5390625
Outputs:
- fisher: float32 [8192, 8192], P('ex', 'tp')
The draws below stay inside these ranges and needn't reach their ends.
All inputs are finite; a program needn't handle non-finite values.
Results may differ from the reference program's by a relative error of at most 0.0003.
Values may be sent and summed in bfloat16 or wider, within the bound.
No kernel may reach another device: no remote copies, remote signals or barrier semaphores. Data moves between devices by JAX's collectives and lax.ppermute only.
A program may use at most 128 MiB of HBM per device.

```python
import jax
import jax.numpy as jnp
from jax import lax

D = 8192
TOK = 128
EXAMPLES = 64


def spiked(entries, stream_key, source, target, shards_of, factor):
    def block_of(axis_at):
        return (jnp.arange(entries.shape[axis_at]) // (entries.shape[axis_at] // shards_of)).reshape((-1,) + (1,) * (entries.ndim - 1 - axis_at))

    one_side = jax.random.permutation(stream_key, shards_of)[block_of(target)]
    far = (block_of(target) + shards_of // 2) % shards_of
    return jnp.where((block_of(source) == one_side) | (block_of(source) == far), factor * entries, entries)


def block_levels(rng, shape, cuts, low, largest):
    loudness = 1.0
    for position, parts in cuts:
        draws = jax.random.uniform(jax.random.fold_in(jax.random.fold_in(rng, 6), position), (parts,), jnp.float32, low / len(cuts), largest / len(cuts))
        loudness = loudness * jnp.repeat(jnp.exp(draws), shape[position] // parts).reshape((-1,) + (1,) * (len(shape) - 1 - position))
    return loudness


def gaussian(stream_key, dims, scale, reach, cuts=(), dtype=jnp.bfloat16):
    result = jax.random.normal(stream_key, dims, jnp.float32) * scale
    if len(cuts) > 0:
        result = block_levels(stream_key, dims, cuts, -0.22, 0.18) * result
    return jnp.clip(result, min=-reach, max=reach).astype(dtype)


def heavy_noise(rng, extent, deviation, most, cuts, heavy, held_as=jnp.bfloat16):
    drawn = deviation * jax.random.normal(rng, extent, jnp.float32)
    if cuts:
        drawn = drawn * block_levels(rng, extent, cuts, -0.22, 0.18)
    return jnp.clip(spiked(drawn, jax.random.fold_in(rng, 3), *heavy), -most, most).astype(held_as)


def setup_inputs(seed: int = 0) -> dict:
    keys = jax.random.split(jax.random.key(seed), 3)
    return {
        "activations": heavy_noise(keys[0], (EXAMPLES, TOK, D), 1.0, 6.0, ((0, 16), (2, 8)), (0, 2, 16, 2.0)),
        "out_grads": gaussian(keys[1], (EXAMPLES, TOK, D), 0.09, 0.5390625, ((0, 16), (2, 8))),
    }


def reference(activations, out_grads):
    def add_example(running, pair):
        inputs_rows, grads_rows = pair
        gradient = jnp.dot(inputs_rows.T, grads_rows, preferred_element_type=jnp.float32)
        return running + gradient * gradient, None

    start_value = jnp.zeros((activations.shape[2], out_grads.shape[2]), jnp.float32)
    fisher, unused = lax.scan(add_example, start_value, (activations, out_grads))
    return fisher
```

```python
import functools

import jax
import jax.numpy as jnp
from jax import lax
from jax.experimental import pallas as pl
from jax.experimental.pallas import tpu as pltpu
from jax.sharding import Mesh, PartitionSpec as P

BF, F32 = jnp.bfloat16, jnp.float32
ANY = pl.BlockSpec(memory_space=pl.ANY)
VM = pl.BlockSpec(memory_space=pltpu.VMEM)
POWER = 12
TOP = 9.625
VMEM_LIMIT = 40 << 20


def ring(n, k):
    return [(i, (i + k) % n) for i in range(n)]


def code_of(u):
    return jnp.where(u == 0, 0, jnp.where(u == 1, 3, jnp.where(u == 2, 1, 2)))


def source_of(code):
    return jnp.where(code == 0, 0, jnp.where(code == 1, 2, jnp.where(code == 2, 3, 1)))


def round_pairs(k):
    pairs = []
    for z in range(4):
        for c in range(2):
            code = [0, 3, 1, 2][(z - 2 * c) % 4] ^ k
            pairs.append((z * 2 + c, (2 * c + code // 2) * 2 + code % 2))
    return pairs


def prep_kernel(a_ref, *o_refs):
    z, c = lax.axis_index("z"), lax.axis_index("c")
    first = code_of(lax.rem(z - 2 * c + 4, 4))
    for k in range(4):
        code = first ^ k
        off = pl.multiple_of(code * 256, 256)
        for e in range(4):
            o_refs[k][e] = a_ref[e, :, pl.ds(off, 256)].T


def prep(a):
    return pl.pallas_call(
        prep_kernel,
        out_shape=[jax.ShapeDtypeStruct((4, 256, 128), BF)] * 4,
        in_specs=[VM],
        out_specs=[VM] * 4,
        compiler_params=pltpu.CompilerParams(vmem_limit_bytes=VMEM_LIMIT),
        name="prep",
    )(a)


def encode(acc, o_ref):
    rows, cols = acc.shape
    top = jnp.max(acc[...], axis=0, keepdims=True)
    top = jnp.max(top, axis=1, keepdims=True)
    k = jnp.clip(jnp.floor(jnp.log2(jnp.maximum(top, 1e-36))), -100.0, 100.0)
    scale = jnp.exp2(TOP - k)
    u = acc[...] * scale
    u2 = u * u
    u4 = u2 * u2
    o_ref[0:rows, :] = (u4 * u4 * u4).astype(BF)
    o_ref[rows : rows + 16, :] = jnp.broadcast_to(k, (16, cols)).astype(BF)


def decode(t, k):
    t = t.astype(F32)
    root = jnp.exp2(jnp.log2(jnp.maximum(t, 1e-38)) * (1.0 / POWER))
    return jnp.where(t > 0, root, 0.0) * jnp.exp2(k.astype(F32) - TOP)


def block_kernel(d, coded, *refs):
    g0, gm, gp, h1, h2, s0, s0c, sm, smc, sp, spc, t1, t1c, t2, t2c, o_ref, a_vm, g_vm, acc_vm, sem = refs
    acc = acc_vm if coded else o_ref
    x, z, y, c = (lax.axis_index(n) for n in "xzyc")
    r = lax.rem(x - y + d + 4, 4)
    a_sem = sem.at[4]
    for slot, src in ((0, g0), (3, gm), (1, gp)):
        pltpu.make_async_copy(src, g_vm.at[slot], sem.at[slot]).start()

    def load(pieces):
        for half, parts in pieces:
            row = pl.multiple_of(half * 256, 256)
            for k, (ref, at) in enumerate(parts):
                u = source_of((2 * lax.rem(z, 2) + half) ^ k)
                slot = lax.rem(u - lax.rem(z, 2) + 4, 4)
                pltpu.make_async_copy(ref.at[pl.ds(at, 4)], a_vm.at[slot, :, pl.ds(row, 256), :], a_sem).start()

    def whole(ref):
        return [(ref, 4 * k) for k in range(4)]

    def parts(one, two):
        return [(one, 0), (one, 4), (two, 0), (two, 4)]

    for value, mine, theirs in ((0, whole(s0), whole(s0c)), (3, whole(sm), whole(smc)), (1, whole(sp), whole(spc)), (2, parts(t1, t2), parts(t1c, t2c))):
        @pl.when(r == value)
        def _():
            load(((c, mine), (1 - c, theirs)))
    pltpu.make_async_copy(h1, g_vm.at[2, 0:2], sem.at[2]).start()
    pltpu.make_async_copy(h2, g_vm.at[2, 2:4], sem.at[5]).start()

    pltpu.make_async_copy(a_vm, a_vm, a_sem).wait()
    for n, slot in enumerate((0, 3, 1, 2)):
        if slot == 2:
            pltpu.make_async_copy(h1, g_vm.at[2, 0:2], sem.at[2]).wait()
            pltpu.make_async_copy(h2, g_vm.at[2, 2:4], sem.at[5]).wait()
        else:
            pltpu.make_async_copy(g0, g_vm.at[slot], sem.at[slot]).wait()

        def tile(t, carry):
            cols = pl.ds(pl.multiple_of(t * 256, 256), 256)
            for i in range(4):
                v = jnp.dot(a_vm[slot, i], g_vm[slot, i, :, cols], preferred_element_type=F32)
                if n == 0 and i == 0:
                    acc[:, cols] = v * v
                else:
                    acc[:, cols] += v * v
            return carry

        lax.fori_loop(0, 4, tile, 0)
    if coded:
        encode(acc, o_ref)


def block(d, coded, refs):
    return pl.pallas_call(
        functools.partial(block_kernel, d, coded),
        out_shape=jax.ShapeDtypeStruct((528, 1024), BF) if coded else jax.ShapeDtypeStruct((512, 1024), F32),
        in_specs=[ANY] * 15,
        out_specs=VM,
        scratch_shapes=[
            pltpu.VMEM((4, 4, 512, 128), BF),
            pltpu.VMEM((4, 4, 128, 1024), BF),
            pltpu.VMEM((512, 1024) if coded else (8, 128), F32),
            pltpu.SemaphoreType.DMA((6,)),
        ],
        compiler_params=pltpu.CompilerParams(vmem_limit_bytes=VMEM_LIMIT),
        cost_estimate=pl.CostEstimate(flops=2 * 16 * 128 * 512 * 1024, bytes_accessed=7 << 20, transcendentals=0),
        name=f"block{d % 4}",
    )(*refs)


def final_kernel(own, p1, p2, p3, k1, k2, k3, o_ref):
    total = own[...]
    for p, k in ((p1, k1), (p2, k2), (p3, k3)):
        total += decode(p[...], k[0:1, 0:1])
    o_ref[...] = total


def final(own, payloads):
    rows = 128
    payload = pl.BlockSpec((rows, 1024), lambda i: (i, 0))
    exponent = pl.BlockSpec((16, 1024), lambda i: (32, 0))
    return pl.pallas_call(
        final_kernel,
        grid=(512 // rows,),
        out_shape=jax.ShapeDtypeStruct((512, 1024), F32),
        in_specs=[payload] * 4 + [exponent] * 3,
        out_specs=payload,
        compiler_params=pltpu.CompilerParams(vmem_limit_bytes=VMEM_LIMIT),
        name="final",
    )(own, *payloads, *payloads)


def body(a, g):
    rounds = [lax.ppermute(p, ("z", "c"), round_pairs(k)) for k, p in enumerate(prep(a))]
    s0 = jnp.concatenate(rounds, axis=0)

    def other(v):
        return lax.ppermute(v, "c", ring(2, 1))

    sm, sp = lax.ppermute(s0, "y", ring(4, 1)), lax.ppermute(s0, "y", ring(4, -1))
    t1, t2 = lax.ppermute(sm[:8], "y", ring(4, 1)), lax.ppermute(sp[8:], "y", ring(4, -1))
    gm, gp = lax.ppermute(g, "z", ring(4, 1)), lax.ppermute(g, "z", ring(4, -1))
    h1, h2 = lax.ppermute(gm[:2], "z", ring(4, 1)), lax.ppermute(gp[2:], "z", ring(4, -1))
    refs = (g, gm, gp, h1, h2, s0, other(s0), sm, other(sm), sp, other(sp), t1, other(t1), t2, other(t2))
    far = lax.ppermute(block(2, True, refs), "x", ring(4, 2))
    right = lax.ppermute(block(1, True, refs), "x", ring(4, 1))
    left = lax.ppermute(block(-1, True, refs), "x", ring(4, -1))
    own = block(0, False, refs)
    return final(own, (far, right, left))


def solution(mesh):
    fine = Mesh(mesh.devices.reshape(4, 4, 4, 2), ("x", "z", "y", "c"))
    spec = P(("x", "z"), None, ("y", "c"))
    return jax.shard_map(body, mesh=fine, in_specs=(spec, spec), out_specs=P(("x", "z"), ("y", "c")), check_vma=False)
```

```python
import functools

import jax
import jax.numpy as jnp
from jax import lax
from jax.experimental import pallas as pl
from jax.experimental.pallas import tpu as pltpu
from jax.sharding import Mesh, PartitionSpec as P

BF, F32 = jnp.bfloat16, jnp.float32
ANY = pl.BlockSpec(memory_space=pl.ANY)
VM = pl.BlockSpec(memory_space=pltpu.VMEM)
POWER = 12
TOP = 9.625
VMEM_LIMIT = 40 << 20


def ring(n, k):
    return [(i, (i + k) % n) for i in range(n)]


def code_of(u):
    return jnp.where(u == 0, 0, jnp.where(u == 1, 3, jnp.where(u == 2, 1, 2)))


def source_of(code):
    return jnp.where(code == 0, 0, jnp.where(code == 1, 2, jnp.where(code == 2, 3, 1)))


def round_pairs(k):
    pairs = []
    for z in range(4):
        for c in range(2):
            code = [0, 3, 1, 2][(z - 2 * c) % 4] ^ k
            pairs.append((z * 2 + c, (2 * c + code // 2) * 2 + code % 2))
    return pairs


def prep_kernel(a_ref, *o_refs):
    z, c = lax.axis_index("z"), lax.axis_index("c")
    first = code_of(lax.rem(z - 2 * c + 4, 4))
    for k in range(4):
        code = first ^ k
        off = pl.multiple_of(code * 256, 256)
        for e in range(4):
            o_refs[k][e] = a_ref[e, :, pl.ds(off, 256)].T


def prep(a):
    return pl.pallas_call(
        prep_kernel,
        out_shape=[jax.ShapeDtypeStruct((4, 256, 128), BF)] * 4,
        in_specs=[VM],
        out_specs=[VM] * 4,
        compiler_params=pltpu.CompilerParams(vmem_limit_bytes=VMEM_LIMIT),
        name="prep",
    )(a)


def encode(acc, o_ref):
    rows, cols = acc.shape
    top = jnp.max(acc[...], axis=0, keepdims=True)
    top = jnp.max(top, axis=1, keepdims=True)
    k = jnp.clip(jnp.floor(jnp.log2(jnp.maximum(top, 1e-36))), -100.0, 100.0)
    scale = jnp.exp2(TOP - k)
    u = acc[...] * scale
    u2 = u * u
    u4 = u2 * u2
    o_ref[0:rows, :] = (u4 * u4 * u4).astype(BF)
    o_ref[rows : rows + 16, :] = jnp.broadcast_to(k, (16, cols)).astype(BF)


def decode(t, k):
    t = t.astype(F32)
    root = jnp.exp2(jnp.log2(jnp.maximum(t, 1e-38)) * (1.0 / POWER))
    return jnp.where(t > 0, root, 0.0) * jnp.exp2(k.astype(F32) - TOP)


SLOTS = (1, 3, 0, 2)


def blocks_kernel(jobs, n_add, *refs):
    n_jobs, halves = len(jobs), sorted({j[1] for j in jobs})
    g_own, a_refs = refs[0], refs[1:17]
    at = 17
    g_refs = refs[at : at + 4]
    at += 4
    adds = refs[at : at + n_add]
    outs = refs[at + n_add : at + n_add + n_jobs]
    a_vm, g_vm, acc_vm, a_sem, g_sem = refs[at + n_add + n_jobs :]
    x, z, y, c = (lax.axis_index(n) for n in "xzyc")

    def start_a(j, d):
        r = lax.rem(x - y + d + 4, 4)
        for value in range(4):
            @pl.when(r == value)
            def _():
                p, q, pc, qc = a_refs[4 * value : 4 * value + 4]
                for half, (first, second) in ((c, (p, q)), (1 - c, (pc, qc))):
                    row = pl.multiple_of(half * 256, 256)
                    for k in (2, 3, 0, 1):
                        u = source_of((2 * lax.rem(z, 2) + half) ^ k)
                        slot = lax.rem(u - lax.rem(z, 2) + 4, 4)
                        src = (first if k >= 2 else second).at[pl.ds((4 * k) % first.shape[0], 4)]
                        pltpu.make_async_copy(src, a_vm.at[j, slot, :, pl.ds(row, 256), :], a_sem.at[j, slot]).start()

    def g_copies(i, h, slot):
        pieces = ((g_refs[2], 0, 2), (g_refs[3], 2, 2)) if slot == 2 else (((g_own, g_refs[1], None, g_refs[0])[slot], 0, 4),)
        return [
            pltpu.make_async_copy(ref.at[:, :, pl.ds(512 * h, 512)], g_vm.at[i, slot, first : first + n], g_sem.at[i, slot + n_th])
            for n_th, (ref, first, n) in zip((0, 2), pieces)
        ]

    for i, h in enumerate(halves):
        if i == 0:
            start_a(0, jobs[0][0])
        for slot in SLOTS:
            for copy in g_copies(i, h, slot):
                copy.start()
    for j in range(1, n_jobs):
        start_a(j, jobs[j][0])
    for j, (d, h, add, coded) in enumerate(jobs):
        i = halves.index(h)
        acc = acc_vm if coded else outs[j]
        for n, slot in enumerate(SLOTS):
            pltpu.make_async_copy(a_vm.at[j, slot], a_vm.at[j, slot], a_sem.at[j, slot]).wait()
            if all(jobs[before][1] != h for before in range(j)):
                for copy in g_copies(i, h, slot):
                    copy.wait()
            for e in range(4):
                v = jnp.dot(a_vm[j, slot, e], g_vm[i, slot, e], preferred_element_type=F32)
                if n == 0 and e == 0:
                    acc[...] = v * v
                else:
                    acc[...] += v * v
        if add is not None:
            acc[...] += decode(adds[add][0:512, :], adds[add][512:513, 0:1])
        if coded:
            encode(acc, outs[j])


def blocks(jobs, g, a_refs, g_refs, adds=()):
    halves = sorted({j[1] for j in jobs})
    n = len(jobs)
    return pl.pallas_call(
        functools.partial(blocks_kernel, jobs, len(adds)),
        out_shape=[jax.ShapeDtypeStruct((528, 512), BF) if j[3] else jax.ShapeDtypeStruct((512, 512), F32) for j in jobs],
        in_specs=[ANY] * 21 + [VM] * len(adds),
        out_specs=[VM] * n,
        scratch_shapes=[
            pltpu.VMEM((n, 4, 4, 512, 128), BF),
            pltpu.VMEM((len(halves), 4, 4, 128, 512), BF),
            pltpu.VMEM((512, 512), F32),
            pltpu.SemaphoreType.DMA((n, 4)),
            pltpu.SemaphoreType.DMA((len(halves), 5)),
        ],
        compiler_params=pltpu.CompilerParams(vmem_limit_bytes=VMEM_LIMIT),
        cost_estimate=pl.CostEstimate(flops=4 * n * 16 * 128 * 512 * 512, bytes_accessed=5 * n << 20, transcendentals=0),
        name="blocks_" + "_".join(f"{d % 4}h{h}" for d, h, _, _ in jobs),
    )(g, *a_refs, *g_refs, *adds)


def final_kernel(own, p1, p2, k1, k2, *rest):
    rest[-1][...] = own[...] + decode(p1[...], k1[0:1, 0:1]) + decode(p2[...], k2[0:1, 0:1])


def final(h, own, one, two, result=None):
    rows = 128
    piece = pl.BlockSpec((rows, 512), lambda i: (i, 0))
    exponent = pl.BlockSpec((16, 512), lambda i: (32, 0))
    return pl.pallas_call(
        final_kernel,
        grid=(512 // rows,),
        out_shape=jax.ShapeDtypeStruct((512, 1024), F32),
        in_specs=[piece] * 3 + [exponent] * 2 + ([] if result is None else [ANY]),
        out_specs=pl.BlockSpec((rows, 512), lambda i: (i, h)),
        input_output_aliases={} if result is None else {5: 0},
        compiler_params=pltpu.CompilerParams(vmem_limit_bytes=VMEM_LIMIT),
        name=f"final{h}",
    )(own, one, two, one, two, *(() if result is None else (result,)))


def send(v, axis, step):
    return lax.ppermute(v, axis, ring(2 if axis == "c" else 4, step))


def after(v, *done):
    return lax.optimization_barrier((v, *done))[0]


def body(a, g):
    rounds = [lax.ppermute(p, ("z", "c"), round_pairs(k)) for k, p in enumerate(prep(a))]
    s = jnp.concatenate(rounds, axis=0)
    sm, sp = send(s, "y", 1), send(s, "y", -1)
    gs = after(g, *rounds)
    gm, gp = send(gs, "z", 1), send(gs, "z", -1)
    sc = send(after(s, *rounds), "c", 1)
    t1, t2 = send(sm[:8], "y", 1), send(sp[8:], "y", -1)
    h1, h2 = send(gm[:2], "z", 1), send(gp[2:], "z", -1)
    smc, spc = send(sm, "c", 1), send(sp, "c", 1)
    t1c, t2c = send(t1, "c", 1), send(t2, "c", 1)
    a_refs = (s, s, sc, sc, sp, sp, spc, spc, t2, t1, t2c, t1c, sm, sm, smc, smc)
    g_refs = (gm, gp, h1, h2)

    def run(jobs, adds=()):
        return blocks(jobs, g, a_refs, g_refs, adds)

    (far1,) = run(((2, 0, None, True),))
    up1 = send(far1, "x", 1)
    (far2,) = run(((2, 1, None, True),))
    up2 = send(far2, "x", -1)
    left1, right2 = run(((-1, 0, None, True), (1, 1, None, True)))
    left1, right2 = send(left1, "x", -1), send(right2, "x", 1)
    (right1,) = run(((1, 0, 0, True),), (up1,))
    right1 = send(right1, "x", 1)
    (left2,) = run(((-1, 1, 0, True),), (up2,))
    left2 = send(left2, "x", -1)
    own1, own2 = run(((0, 0, None, False), (0, 1, None, False)))
    return final(1, own2, left2, right2, final(0, own1, left1, right1))


def solution(mesh):
    fine = Mesh(mesh.devices.reshape(4, 4, 4, 2), ("x", "z", "y", "c"))
    spec = P(("x", "z"), None, ("y", "c"))
    return jax.shard_map(body, mesh=fine, in_specs=(spec, spec), out_specs=P(("x", "z"), ("y", "c")), check_vma=False)
```

```python
import functools

import jax
import jax.numpy as jnp
from jax import lax
from jax.experimental import pallas as pl
from jax.experimental.pallas import tpu as pltpu
from jax.sharding import Mesh, PartitionSpec as P

BF, F32 = jnp.bfloat16, jnp.float32
ANY = pl.BlockSpec(memory_space=pl.ANY)
VM = pl.BlockSpec(memory_space=pltpu.VMEM)
POWER = 12
TOP = 9.625
VMEM_LIMIT = 16 << 20


def ring(n, k):
    return [(i, (i + k) % n) for i in range(n)]


def code_of(u):
    return jnp.where(u == 0, 0, jnp.where(u == 1, 3, jnp.where(u == 2, 1, 2)))


def source_of(code):
    return jnp.where(code == 0, 0, jnp.where(code == 1, 2, jnp.where(code == 2, 3, 1)))


def round_pairs(k):
    pairs = []
    for z in range(4):
        for c in range(2):
            code = [0, 3, 1, 2][(z - 2 * c) % 4] ^ (2 * k)
            pairs.append((z * 2 + c, (2 * c + code // 2) * 2 + code % 2))
    return pairs


def prep_kernel(a_ref, *o_refs):
    z, c = lax.axis_index("z"), lax.axis_index("c")
    first = code_of(lax.rem(z - 2 * c + 4, 4))
    for k in range(2):
        off = pl.multiple_of(((first ^ (2 * k)) // 2) * 512, 512)
        o_refs[k][0] = a_ref[0, :, pl.ds(off, 512)].T


def prep(a):
    return pl.pallas_call(
        prep_kernel,
        grid=(4,),
        out_shape=[jax.ShapeDtypeStruct((4, 512, 128), BF)] * 2,
        in_specs=[pl.BlockSpec((1, 128, 1024), lambda e: (e, 0, 0))],
        out_specs=[pl.BlockSpec((1, 512, 128), lambda e: (e, 0, 0))] * 2,
        compiler_params=pltpu.CompilerParams(vmem_limit_bytes=VMEM_LIMIT),
        name="prep",
    )(a)


def encode(acc, o_ref):
    rows, cols = acc.shape
    step = 32

    def largest(i, top):
        part = acc[pl.ds(pl.multiple_of(i * step, step), step), :].reshape(step // 8, 8, cols)
        return jnp.maximum(top, jnp.max(part, axis=0))

    top = lax.fori_loop(0, rows // step, largest, jnp.zeros((8, cols), F32))
    top = jnp.max(jnp.max(top, axis=0, keepdims=True), axis=1, keepdims=True)
    k = jnp.clip(jnp.floor(jnp.log2(jnp.maximum(top, 1e-36))), -100.0, 100.0)
    scale = jnp.exp2(TOP - k)

    def power(u):
        u2 = u * u
        u4 = u2 * u2
        return u4 * u4 * u4

    @pl.loop(0, rows // step)
    def _(i):
        at = pl.ds(pl.multiple_of(i * step, step), step)
        o_ref[at, :] = power(acc[at, :] * scale).astype(BF)

    lane, row = (lax.broadcasted_iota(jnp.int32, (16, 128), d) for d in (1, 0))
    shifted = jnp.floor((k + 128.0) * jnp.exp2(-lane.astype(F32)))
    odd = (shifted - 2.0 * jnp.floor(0.5 * shifted)) > 0.5
    t = power(acc[0:16, 0:128] * scale)
    coded = jnp.where(odd, -1.0, 1.0) * jnp.maximum(t, 1e-37)
    o_ref[0:16, 0:128] = jnp.where((row == 0) & (lane < 8), coded, t).astype(BF)


def exponent(p_ref):
    lane, row = (lax.broadcasted_iota(jnp.int32, (16, 128), d) for d in (1, 0))
    bit = (row == 0) & (lane < 8) & (p_ref[0:16, 0:128].astype(F32) < 0)
    value = jnp.where(bit, jnp.exp2(lane.astype(F32)), 0.0)
    return jnp.sum(jnp.sum(value, axis=0, keepdims=True), axis=1, keepdims=True) - 128.0


def decode(t, k):
    t = jnp.abs(t.astype(F32))
    root = jnp.exp2(jnp.log2(jnp.maximum(t, 1e-38)) * (1.0 / POWER))
    return jnp.where(t > 0, root, 0.0) * jnp.exp2(k - TOP)


def gather_kernel(g, gp, h1, h2, gm, o_ref, sem):
    copies = [pltpu.make_async_copy(src, o_ref.at[slot], sem.at[slot]) for slot, src in ((0, g), (1, gp), (3, gm))]
    copies += [pltpu.make_async_copy(src, o_ref.at[2, pl.ds(2 * i, 2)], sem.at[2 + 2 * i]) for i, src in enumerate((h1, h2))]
    for copy in copies:
        copy.start()
    for copy in copies:
        copy.wait()


def gather(*pieces):
    return pl.pallas_call(
        gather_kernel,
        out_shape=jax.ShapeDtypeStruct((4, 4, 128, 1024), BF),
        in_specs=[ANY] * 5,
        out_specs=VM,
        scratch_shapes=[pltpu.SemaphoreType.DMA((5,))],
        compiler_params=pltpu.CompilerParams(vmem_limit_bytes=16 << 20),
        name="gather",
    )(*pieces)


OWN = (((0, 0), (0, 4)), ((2, 0), (2, 4)), ((3, 0), (4, 0)), ((1, 0), (1, 4)))
OTHER = (((5, 0), (5, 4)), ((6, 8), (6, 12)), ((7, 0), (7, 4)), ((6, 0), (6, 4)))


ALL, MINE, THEIRS = (0, 1, 2, 3), (0, 1), (2, 3)
ROWS = (288, 224)


def blocks_kernel(jobs, n_extra, *refs):
    n = len(jobs)
    a_refs, g_ref = refs[:8], refs[8]
    extra = refs[9 : 9 + n_extra]
    outs = refs[9 + n_extra : 9 + n_extra + n]
    a_vm, acc_vm, sem = refs[9 + n_extra + n :]
    x, z, y, c = (lax.axis_index(name) for name in "xzyc")
    odd = lax.rem(z, 2)
    for j, (d, first_row, rows, _, _, _, pieces) in enumerate(jobs):
        r = lax.rem(x - y + d + 4, 4)
        for value in range(4):
            @pl.when(r == value)
            def _():
                for piece in pieces:
                    ref, first = (OWN[value] + OTHER[value])[piece]
                    src = a_refs[ref].at[pl.ds(first, 4), pl.ds(first_row, rows), :]
                    pltpu.make_async_copy(src, a_vm.at[j, piece, :, 0:rows, :], sem.at[j, piece]).start()
    for j, (_, first_row, rows, begin, add, coded, pieces) in enumerate(jobs):
        acc = acc_vm.at[0:rows] if coded else outs[j]
        if begin is None:
            acc[...] = jnp.zeros_like(acc)
        else:
            acc[...] = extra[begin][first_row : first_row + rows, :]

        @pl.loop(pieces[0], pieces[-1] + 1)
        def _(piece):
            core = jnp.where(piece < 2, c, 1 - c)
            slot = lax.rem(source_of((2 * odd + core) ^ (2 * lax.rem(piece, 2))) - odd + 4, 4)
            held = a_vm.at[j, piece, :, 0:rows, :]
            pltpu.make_async_copy(held, held, sem.at[j, piece]).wait()
            for e in range(4):
                v = jnp.dot(a_vm[j, piece, e, 0:rows, :], g_ref[slot, e], preferred_element_type=F32)
                acc[...] += v * v

        if add is not None:
            k = exponent(extra[add])

            @pl.loop(0, rows // 32)
            def _(i):
                at = pl.ds(pl.multiple_of(i * 32, 32), 32)
                acc[at, :] += decode(extra[add][at, :], k)

        if coded:
            encode(acc, outs[j])


def blocks(jobs, a_refs, g, extra=()):
    n = len(jobs)
    most = max(j[2] for j in jobs)
    return pl.pallas_call(
        functools.partial(blocks_kernel, jobs, len(extra)),
        out_shape=[jax.ShapeDtypeStruct((j[2], 1024), BF if j[5] else F32) for j in jobs],
        in_specs=[ANY] * 8 + [VM] * (1 + len(extra)),
        out_specs=[VM] * n,
        scratch_shapes=[
            pltpu.VMEM((n, 4, 4, most, 128), BF),
            pltpu.VMEM((most, 1024), F32),
            pltpu.SemaphoreType.DMA((n, 4)),
        ],
        compiler_params=pltpu.CompilerParams(vmem_limit_bytes=VMEM_LIMIT),
        cost_estimate=pl.CostEstimate(flops=4 * n * 16 * 128 * 512 * 512, bytes_accessed=5 * n << 20, transcendentals=0),
        name="blocks_" + "_".join(f"{j[0] % 4}r{j[1]}" for j in jobs),
    )(*a_refs, g, *extra)


def final_kernel(part, own, p1, p2, *rest):
    o_ref, tmp, sem = rest[-3:]
    rows = ROWS[part]
    k1, k2 = exponent(p1), exponent(p2)

    @pl.loop(0, rows // 32)
    def _(i):
        at = pl.ds(pl.multiple_of(i * 32, 32), 32)
        tmp[at, :] = own[at, :] + decode(p1[at, :], k1) + decode(p2[at, :], k2)
        to = pl.ds(pl.multiple_of(ROWS[0] * part + i * 32, 32), 32)
        pltpu.make_async_copy(tmp.at[at], o_ref.at[to], sem).start()

    pltpu.make_async_copy(tmp, tmp, sem).wait()


def final(part, own, one, two, result=None):
    return pl.pallas_call(
        functools.partial(final_kernel, part),
        out_shape=jax.ShapeDtypeStruct((512, 1024), F32),
        in_specs=[VM] * 3 + ([] if result is None else [ANY]),
        out_specs=ANY,
        scratch_shapes=[pltpu.VMEM((ROWS[part], 1024), F32), pltpu.SemaphoreType.DMA],
        input_output_aliases={} if result is None else {3: 0},
        compiler_params=pltpu.CompilerParams(vmem_limit_bytes=VMEM_LIMIT),
        name=f"final{part}",
    )(own, one, two, *(() if result is None else (result,)))


def send(v, axis, step):
    return lax.ppermute(v, axis, ring(2 if axis == "c" else 4, step))


def body(a, g):
    r0, r1 = (lax.ppermute(p, ("z", "c"), round_pairs(k)) for k, p in enumerate(prep(a)))
    r0, r1, g = lax.optimization_barrier((r0, r1, g))
    s = jnp.concatenate([r0, r1], axis=0)
    sm, sp, gm, gp, sc = send(s, "y", 1), send(s, "y", -1), send(g, "z", 1), send(g, "z", -1), send(s, "c", 1)
    sm, sp, gm, gp, sc = lax.optimization_barrier((sm, sp, gm, gp, sc))
    t1, t2 = send(sm[:4], "y", 1), send(sp[4:], "y", -1)
    h1, h2 = send(gm[:2], "z", 1), send(gp[2:], "z", -1)
    both = send(jnp.concatenate([sm, sp], axis=0), "c", 1)
    t1, t2, h1, h2, both = lax.optimization_barrier((t1, t2, h1, h2, both))
    tc = send(jnp.concatenate([t1, t2], axis=0), "c", 1)
    gs = gather(g, gp, h1, h2, gm)
    a_refs = (s, sm, sp, t1, t2, sc, both, tc)

    def run(jobs, extra=()):
        return blocks(jobs, a_refs, gs, extra)

    def job(d, part, add=None, coded=True):
        return (d, ROWS[0] * part, ROWS[part], None, add, coded, ALL)

    (early,) = blocks(((2, 0, 512, None, None, False, MINE),), (*a_refs[:5], s, s, s), gs)
    (far0,) = run(((2, 0, ROWS[0], 0, None, True, THEIRS),), (early,))
    up0 = send(far0, "x", 1)
    (far1,) = run(((2, ROWS[0], ROWS[1], 0, None, True, THEIRS),), (early,))
    up1 = send(far1, "x", -1)
    left0, right1 = run((job(-1, 0), job(1, 1)))
    left0, right1 = send(left0, "x", -1), send(right1, "x", 1)
    (right0,) = run((job(1, 0, 0),), (up0,))
    right0 = send(right0, "x", 1)
    (left1,) = run((job(-1, 1, 0),), (up1,))
    left1 = send(left1, "x", -1)
    own0, own1 = run((job(0, 0, coded=False), job(0, 1, coded=False)))
    return final(1, own1, left1, right1, final(0, own0, left0, right0))


def solution(mesh):
    fine = Mesh(mesh.devices.reshape(4, 4, 4, 2), ("x", "z", "y", "c"))
    spec = P(("x", "z"), None, ("y", "c"))
    return jax.shard_map(body, mesh=fine, in_specs=(spec, spec), out_specs=P(("x", "z"), ("y", "c")), check_vma=False)
```

```python
import functools

import jax
import jax.numpy as jnp
from jax import lax
from jax.experimental import pallas as pl
from jax.experimental.pallas import tpu as pltpu
from jax.sharding import Mesh, PartitionSpec as P

BF, F32 = jnp.bfloat16, jnp.float32
ANY = pl.BlockSpec(memory_space=pl.ANY)
VM = pl.BlockSpec(memory_space=pltpu.VMEM)
POWER = 12
TOP = 9.625
VMEM_LIMIT = 16 << 20


def ring(n, k):
    return [(i, (i + k) % n) for i in range(n)]


def code_of(u):
    return jnp.where(u == 0, 0, jnp.where(u == 1, 3, jnp.where(u == 2, 1, 2)))


def source_of(code):
    return jnp.where(code == 0, 0, jnp.where(code == 1, 2, jnp.where(code == 2, 3, 1)))


def round_pairs(k):
    pairs = []
    for z in range(4):
        for c in range(2):
            code = [0, 3, 1, 2][(z - 2 * c) % 4] ^ (2 * k)
            pairs.append((z * 2 + c, (2 * c + code // 2) * 2 + code % 2))
    return pairs


def prep_kernel(a_ref, o0_ref, o1_ref, a_vm, sem):
    z, c = lax.axis_index("z"), lax.axis_index("c")
    first = code_of(lax.rem(z - 2 * c + 4, 4))
    copies = [pltpu.make_async_copy(a_ref.at[e], a_vm.at[e], sem.at[e]) for e in range(4)]
    for copy in copies:
        copy.start()
    for e in range(4):
        copies[e].wait()
        for k, o_ref in enumerate((o0_ref, o1_ref)):
            off = pl.multiple_of(((first ^ (2 * k)) // 2) * 512, 512)
            o_ref[e] = a_vm[e, :, pl.ds(off, 512)].T


def prep(a):
    return pl.pallas_call(
        prep_kernel,
        out_shape=[jax.ShapeDtypeStruct((4, 512, 128), BF)] * 2,
        in_specs=[pl.BlockSpec(memory_space=pltpu.HBM)],
        out_specs=[VM] * 2,
        scratch_shapes=[pltpu.VMEM((4, 128, 1024), BF), pltpu.SemaphoreType.DMA((4,))],
        compiler_params=pltpu.CompilerParams(vmem_limit_bytes=VMEM_LIMIT),
        name="prep",
    )(a)


def encode(acc, o_ref):
    rows, cols = acc.shape
    step = 16

    def largest(i, top):
        part = acc[pl.ds(pl.multiple_of(i * step, step), step), :].reshape(step // 8, 8, cols)
        return jnp.maximum(top, jnp.max(part, axis=0))

    top = lax.fori_loop(0, rows // step, largest, jnp.zeros((8, cols), F32))
    top = jnp.max(jnp.max(top, axis=0, keepdims=True), axis=1, keepdims=True)
    k = jnp.clip(jnp.floor(jnp.log2(jnp.maximum(top, 1e-36))), -100.0, 100.0)
    scale = jnp.exp2(TOP - k)

    def power(u):
        u2 = u * u
        u4 = u2 * u2
        return u4 * u4 * u4

    @pl.loop(0, rows // step)
    def _(i):
        at = pl.ds(pl.multiple_of(i * step, step), step)
        o_ref[at, :] = power(acc[at, :] * scale).astype(BF)

    lane, row = (lax.broadcasted_iota(jnp.int32, (16, 128), d) for d in (1, 0))
    shifted = jnp.floor((k + 128.0) * jnp.exp2(-lane.astype(F32)))
    odd = (shifted - 2.0 * jnp.floor(0.5 * shifted)) > 0.5
    t = power(acc[0:16, 0:128] * scale)
    coded = jnp.where(odd, -1.0, 1.0) * jnp.maximum(t, 1e-37)
    o_ref[0:16, 0:128] = jnp.where((row == 0) & (lane < 8), coded, t).astype(BF)


def exponent(p_ref):
    lane, row = (lax.broadcasted_iota(jnp.int32, (16, 128), d) for d in (1, 0))
    bit = (row == 0) & (lane < 8) & (p_ref[0:16, 0:128].astype(F32) < 0)
    value = jnp.where(bit, jnp.exp2(lane.astype(F32)), 0.0)
    return jnp.sum(jnp.sum(value, axis=0, keepdims=True), axis=1, keepdims=True) - 128.0


def decode(t, k):
    t = jnp.abs(t.astype(F32))
    root = jnp.exp2(jnp.log2(jnp.maximum(t, 1e-38)) * (1.0 / POWER))
    return jnp.where(t > 0, root, 0.0) * jnp.exp2(k - TOP)


def gather_kernel(g, za, zb, zac, zbc, fa, fb, o_ref, sem):
    c = lax.axis_index("c")
    near, far = jnp.where(c == 0, 3, 1), jnp.where(c == 0, 1, 3)
    copies = [
        pltpu.make_async_copy(g, o_ref.at[0], sem.at[0]),
        pltpu.make_async_copy(za.at[0], o_ref.at[near, 0:2], sem.at[1]),
        pltpu.make_async_copy(zb.at[0], o_ref.at[near, 2:4], sem.at[2]),
        pltpu.make_async_copy(zac, o_ref.at[far, 0:2], sem.at[3]),
        pltpu.make_async_copy(zbc, o_ref.at[far, 2:4], sem.at[6]),
        pltpu.make_async_copy(fa, o_ref.at[2, 0:2], sem.at[4]),
        pltpu.make_async_copy(fb, o_ref.at[2, 2:4], sem.at[5]),
    ]
    for copy in copies:
        copy.start()
    for copy in copies:
        copy.wait()


def gather(*pieces):
    return pl.pallas_call(
        gather_kernel,
        out_shape=jax.ShapeDtypeStruct((4, 4, 128, 1024), BF),
        in_specs=[ANY] * 7,
        out_specs=VM,
        scratch_shapes=[pltpu.SemaphoreType.DMA((7,))],
        compiler_params=pltpu.CompilerParams(vmem_limit_bytes=VMEM_LIMIT),
        name="gather",
    )(*pieces)


PIECES = {
    (0, None): ((0, 0), (1, 0), (2, 0), (3, 0)),
    (2, None): ((8, 0), (9, 0), (10, 0), (10, 4)),
    (3, 0): ((4, 0), (5, 0), (4, 4), (5, 4)),
    (3, 1): ((6, 4), (7, 4), (6, 0), (7, 0)),
    (1, 0): ((6, 4), (7, 4), (6, 0), (7, 0)),
    (1, 1): ((4, 0), (5, 0), (4, 4), (5, 4)),
}
ALL, MINE, THEIRS = (0, 1, 2, 3), (0, 1), (2, 3)
ROWS = (272, 240)


def blocks_kernel(jobs, n_extra, *refs):
    n = len(jobs)
    a_refs, g_ref = refs[:11], refs[11]
    extra = refs[12 : 12 + n_extra]
    outs = refs[12 + n_extra : 12 + n_extra + n]
    a_vm, acc_vm, sem = refs[12 + n_extra + n :]
    x, z, y, c = (lax.axis_index(name) for name in "xzyc")
    odd = lax.rem(z, 2)
    for j, (d, first_row, rows, _, _, _, pieces) in enumerate(jobs):
        r = lax.rem(x - y + d + 4, 4)
        for (value, on_core), places in PIECES.items():
            @pl.when(r == value if on_core is None else (r == value) & (c == on_core))
            def _():
                for piece in pieces:
                    ref, first = places[piece]
                    src = a_refs[ref].at[pl.ds(first, 4), pl.ds(first_row, rows), :]
                    pltpu.make_async_copy(src, a_vm.at[j, piece, :, 0:rows, :], sem.at[j, piece]).start()
    for j, (_, first_row, rows, begin, add, coded, pieces) in enumerate(jobs):
        acc = acc_vm.at[0:rows] if coded else outs[j]
        if begin is None:
            acc[...] = jnp.zeros_like(acc)
        else:
            acc[...] = extra[begin][first_row : first_row + rows, :]

        @pl.loop(pieces[0], pieces[-1] + 1)
        def _(piece):
            core = jnp.where(piece < 2, c, 1 - c)
            slot = lax.rem(source_of((2 * odd + core) ^ (2 * lax.rem(piece, 2))) - odd + 4, 4)
            held = a_vm.at[j, piece, :, 0:rows, :]
            pltpu.make_async_copy(held, held, sem.at[j, piece]).wait()
            for e in range(4):
                v = jnp.dot(a_vm[j, piece, e, 0:rows, :], g_ref[slot, e], preferred_element_type=F32)
                acc[...] += v * v

        if add is not None:
            k = exponent(extra[add])

            @pl.loop(0, rows // 16)
            def _(i):
                at = pl.ds(pl.multiple_of(i * 16, 16), 16)
                acc[at, :] += decode(extra[add][at, :], k)

        if coded:
            encode(acc, outs[j])


def blocks(jobs, a_refs, g, extra=()):
    n = len(jobs)
    most = max(j[2] for j in jobs)
    return pl.pallas_call(
        functools.partial(blocks_kernel, jobs, len(extra)),
        out_shape=[jax.ShapeDtypeStruct((j[2], 1024), BF if j[5] else F32) for j in jobs],
        in_specs=[ANY] * 11 + [VM] * (1 + len(extra)),
        out_specs=[VM] * n,
        scratch_shapes=[
            pltpu.VMEM((n, 4, 4, most, 128), BF),
            pltpu.VMEM((most, 1024), F32),
            pltpu.SemaphoreType.DMA((n, 4)),
        ],
        compiler_params=pltpu.CompilerParams(vmem_limit_bytes=VMEM_LIMIT),
        cost_estimate=pl.CostEstimate(flops=4 * n * 16 * 128 * 512 * 512, bytes_accessed=5 * n << 20, transcendentals=0),
        name="blocks_" + "_".join(f"{j[0] % 4}r{j[1]}" for j in jobs),
    )(*a_refs, g, *extra)


def final_kernel(part, own, p, *rest):
    o_ref, tmp, sem = rest[-3:]
    rows = ROWS[part]
    k = exponent(p)

    @pl.loop(0, rows // 16)
    def _(i):
        at = pl.ds(pl.multiple_of(i * 16, 16), 16)
        tmp[at, :] = own[at, :] + decode(p[at, :], k)
        to = pl.ds(pl.multiple_of(ROWS[0] * part + i * 16, 16), 16)
        pltpu.make_async_copy(tmp.at[at], o_ref.at[to], sem).start()

    pltpu.make_async_copy(tmp, tmp, sem).wait()


def final(part, own, payload, result=None):
    return pl.pallas_call(
        functools.partial(final_kernel, part),
        out_shape=jax.ShapeDtypeStruct((512, 1024), F32),
        in_specs=[VM] * 2 + ([] if result is None else [ANY]),
        out_specs=ANY,
        scratch_shapes=[pltpu.VMEM((ROWS[part], 1024), F32), pltpu.SemaphoreType.DMA],
        input_output_aliases={} if result is None else {2: 0},
        compiler_params=pltpu.CompilerParams(vmem_limit_bytes=VMEM_LIMIT),
        name=f"final{part}",
    )(own, payload, *(() if result is None else (result,)))


def send(v, axis, step):
    return lax.ppermute(v, axis, ring(2 if axis == "c" else 4, step))


def both_ways(v, axis):
    pairs = [(2 * i, 2 * ((i + 1) % 4)) for i in range(4)] + [(2 * i + 1, 2 * ((i + 3) % 4) + 1) for i in range(4)]
    return lax.ppermute(v, (axis, "c"), pairs)


def cross(v):
    return send(v, "c", 1)


def body(a, g):
    hold = lax.optimization_barrier
    gc = cross(g)
    r0, r1 = (lax.ppermute(p, ("z", "c"), round_pairs(k)) for k, p in enumerate(prep(a)))
    r0, r1, gc = hold((r0, r1, gc))
    r1c, r0c = cross(r1), cross(r0)
    za = both_ways(jnp.stack([g[:2], gc[:2]]), "z")
    zb = both_ways(jnp.stack([g[2:], gc[2:]]), "z")
    m1 = both_ways(jnp.concatenate([r1, r1c]), "y")
    m0 = both_ways(jnp.concatenate([r0, r0c]), "y")
    m1, za = hold((m1, za))
    f1, fa, m1c = both_ways(m1[:4], "y"), both_ways(za[0], "z"), cross(m1)
    zac = cross(za[1])
    m0, zb, m1c, zac = hold((m0, zb, m1c, zac))
    f0, fb, m0c = both_ways(m0[:4], "y"), both_ways(zb[0], "z"), cross(m0)
    f1, zbh = hold((f1, zb[1]))
    zbc = cross(zbh)
    f0, f1, fa, fb, m0c, zac, zbc = hold((f0, f1, fa, fb, m0c, zac, zbc))
    fc = cross(jnp.concatenate([f0, f1]))
    gs = gather(g, za, zb, zac, zbc, fa, fb)
    a_refs = (r0, r1, r0c, r1c, m0, m1, m0c, m1c, f0, f1, fc)

    def run(jobs, extra=()):
        return blocks(jobs, a_refs, gs, extra)

    def job(d, part, add=None, coded=True):
        return (d, ROWS[0] * part, ROWS[part], None, add, coded, ALL)

    (early,) = blocks(((2, 0, 512, None, None, False, MINE),), (*a_refs[:10], r0), gs)
    (far0,) = run(((2, 0, ROWS[0], 0, None, True, THEIRS),), (early,))
    up0 = send(far0, "x", 1)
    (far1,) = run(((2, ROWS[0], ROWS[1], 0, None, True, THEIRS),), (early,))
    up1 = send(far1, "x", -1)
    (left0,) = run((job(-1, 0),))
    left0 = send(left0, "x", -1)
    (right1,) = run((job(1, 1),))
    right1 = send(right1, "x", 1)
    (right0,) = run((job(1, 0, 0),), (up0,))
    right0 = send(right0, "x", 1)
    (left1,) = run((job(-1, 1, 0),), (up1,))
    left1 = send(left1, "x", -1)
    (own1,) = run((job(0, 1, 0, False),), (right1,))
    (own0,) = run((job(0, 0, 0, False),), (left0,))
    return final(1, own1, left1, final(0, own0, right0))


def solution(mesh):
    fine = Mesh(mesh.devices.reshape(4, 4, 4, 2), ("x", "z", "y", "c"))
    spec = P(("x", "z"), None, ("y", "c"))
    return jax.shard_map(body, mesh=fine, in_specs=(spec, spec), out_specs=P(("x", "z"), ("y", "c")), check_vma=False)
```

```python
import functools

import jax
import jax.numpy as jnp
from jax import lax
from jax.experimental import pallas as pl
from jax.experimental.pallas import tpu as pltpu
from jax.sharding import Mesh, PartitionSpec as P

BF, F32 = jnp.bfloat16, jnp.float32
ANY = pl.BlockSpec(memory_space=pl.ANY)
VM = pl.BlockSpec(memory_space=pltpu.VMEM)
POWER = 12
TOP = 9.625
VMEM_LIMIT = 16 << 20


def ring(n, k):
    return [(i, (i + k) % n) for i in range(n)]


def code_of(u):
    return jnp.where(u == 0, 0, jnp.where(u == 1, 3, jnp.where(u == 2, 1, 2)))


def source_of(code):
    return jnp.where(code == 0, 0, jnp.where(code == 1, 2, jnp.where(code == 2, 3, 1)))


def round_pairs(k):
    pairs = []
    for z in range(4):
        for c in range(2):
            code = [0, 3, 1, 2][(z - 2 * c) % 4] ^ (2 * k)
            pairs.append((z * 2 + c, (2 * c + code // 2) * 2 + code % 2))
    return pairs


def prep_kernel(k, a_ref, *rest):
    o_ref, a_vm, sem = rest[-3:]
    z, c = lax.axis_index("z"), lax.axis_index("c")
    code = code_of(lax.rem(z - 2 * c + 4, 4)) ^ (2 * k)
    off = pl.multiple_of((code // 2) * 512, 512)
    copies = [pltpu.make_async_copy(a_ref.at[e, :, pl.ds(off, 512)], a_vm.at[e], sem.at[e]) for e in range(4)]
    for copy in copies:
        copy.start()
    for e in range(4):
        copies[e].wait()
        o_ref[e] = a_vm[e].T


def prep(k, a, *before):
    return pl.pallas_call(
        functools.partial(prep_kernel, k),
        out_shape=jax.ShapeDtypeStruct((4, 512, 128), BF),
        in_specs=[ANY] * (1 + len(before)),
        out_specs=VM,
        scratch_shapes=[pltpu.VMEM((4, 128, 512), BF), pltpu.SemaphoreType.DMA((4,))],
        compiler_params=pltpu.CompilerParams(vmem_limit_bytes=VMEM_LIMIT),
        name=f"prep{k}",
    )(a, *before)


def encode(acc, o_ref):
    rows, cols = acc.shape
    step = 16

    def largest(i, top):
        part = acc[pl.ds(pl.multiple_of(i * step, step), step), :].reshape(step // 8, 8, cols)
        return jnp.maximum(top, jnp.max(part, axis=0))

    top = lax.fori_loop(0, rows // step, largest, jnp.zeros((8, cols), F32))
    top = jnp.max(jnp.max(top, axis=0, keepdims=True), axis=1, keepdims=True)
    k = jnp.clip(jnp.floor(jnp.log2(jnp.maximum(top, 1e-36))), -100.0, 100.0)
    scale = jnp.exp2(TOP - k)

    def power(u):
        u2 = u * u
        u4 = u2 * u2
        return u4 * u4 * u4

    @pl.loop(0, rows // step)
    def _(i):
        at = pl.ds(pl.multiple_of(i * step, step), step)
        o_ref[at, :] = power(acc[at, :] * scale).astype(BF)

    lane, row = (lax.broadcasted_iota(jnp.int32, (16, 128), d) for d in (1, 0))
    shifted = jnp.floor((k + 128.0) * jnp.exp2(-lane.astype(F32)))
    odd = (shifted - 2.0 * jnp.floor(0.5 * shifted)) > 0.5
    t = power(acc[0:16, 0:128] * scale)
    coded = jnp.where(odd, -1.0, 1.0) * jnp.maximum(t, 1e-37)
    o_ref[0:16, 0:128] = jnp.where((row == 0) & (lane < 8), coded, t).astype(BF)


def exponent(p_ref):
    lane, row = (lax.broadcasted_iota(jnp.int32, (16, 128), d) for d in (1, 0))
    bit = (row == 0) & (lane < 8) & (p_ref[0:16, 0:128].astype(F32) < 0)
    value = jnp.where(bit, jnp.exp2(lane.astype(F32)), 0.0)
    return jnp.sum(jnp.sum(value, axis=0, keepdims=True), axis=1, keepdims=True) - 128.0


def decode(t, k):
    t = jnp.abs(t.astype(F32))
    root = jnp.exp2(jnp.log2(jnp.maximum(t, 1e-38)) * (1.0 / POWER))
    return jnp.where(t > 0, root, 0.0) * jnp.exp2(k - TOP)


def gather_kernel(g, za, zb, zac, zbc, fa, fb, o_ref, sem):
    c = lax.axis_index("c")
    near, far = jnp.where(c == 0, 3, 1), jnp.where(c == 0, 1, 3)
    copies = [
        pltpu.make_async_copy(g, o_ref.at[0], sem.at[0]),
        pltpu.make_async_copy(za.at[0], o_ref.at[near, 0:2], sem.at[1]),
        pltpu.make_async_copy(zb.at[0], o_ref.at[near, 2:4], sem.at[2]),
        pltpu.make_async_copy(zac, o_ref.at[far, 0:2], sem.at[3]),
        pltpu.make_async_copy(zbc, o_ref.at[far, 2:4], sem.at[6]),
        pltpu.make_async_copy(fa, o_ref.at[2, 0:2], sem.at[4]),
        pltpu.make_async_copy(fb, o_ref.at[2, 2:4], sem.at[5]),
    ]
    for copy in copies:
        copy.start()
    for copy in copies:
        copy.wait()


def gather(*pieces):
    return pl.pallas_call(
        gather_kernel,
        out_shape=jax.ShapeDtypeStruct((4, 4, 128, 1024), BF),
        in_specs=[ANY] * 7,
        out_specs=VM,
        scratch_shapes=[pltpu.SemaphoreType.DMA((7,))],
        compiler_params=pltpu.CompilerParams(vmem_limit_bytes=VMEM_LIMIT),
        name="gather",
    )(*pieces)


PIECES = {
    (0, None): ((0, 0), (1, 0), (2, 0), (3, 0)),
    (2, None): ((8, 0), (9, 0), (10, 0), (10, 4)),
    (3, 0): ((4, 0), (5, 0), (4, 4), (5, 4)),
    (3, 1): ((6, 4), (7, 4), (6, 0), (7, 0)),
    (1, 0): ((6, 4), (7, 4), (6, 0), (7, 0)),
    (1, 1): ((4, 0), (5, 0), (4, 4), (5, 4)),
}
ALL, MINE, THEIRS = (0, 1, 2, 3), (0, 1), (2, 3)
ROWS = (272, 240)


def blocks_kernel(jobs, n_extra, *refs):
    n = len(jobs)
    a_refs, g_ref = refs[:11], refs[11]
    extra = refs[12 : 12 + n_extra]
    outs = refs[12 + n_extra : 12 + n_extra + n]
    a_vm, acc_vm, sem = refs[12 + n_extra + n :]
    x, z, y, c = (lax.axis_index(name) for name in "xzyc")
    odd = lax.rem(z, 2)
    for j, (d, first_row, rows, _, _, _, pieces) in enumerate(jobs):
        r = lax.rem(x - y + d + 4, 4)
        for (value, on_core), places in PIECES.items():
            @pl.when(r == value if on_core is None else (r == value) & (c == on_core))
            def _():
                for piece in pieces:
                    ref, first = places[piece]
                    src = a_refs[ref].at[pl.ds(first, 4), pl.ds(first_row, rows), :]
                    pltpu.make_async_copy(src, a_vm.at[j, piece, :, 0:rows, :], sem.at[j, piece]).start()
    for j, (_, first_row, rows, begin, add, coded, pieces) in enumerate(jobs):
        acc = acc_vm.at[0:rows] if coded else outs[j]
        if begin is None:
            acc[...] = jnp.zeros_like(acc)
        else:
            acc[...] = extra[begin][first_row : first_row + rows, :]

        @pl.loop(pieces[0], pieces[-1] + 1)
        def _(piece):
            core = jnp.where(piece < 2, c, 1 - c)
            slot = lax.rem(source_of((2 * odd + core) ^ (2 * lax.rem(piece, 2))) - odd + 4, 4)
            held = a_vm.at[j, piece, :, 0:rows, :]
            pltpu.make_async_copy(held, held, sem.at[j, piece]).wait()
            for e in range(4):
                v = jnp.dot(a_vm[j, piece, e, 0:rows, :], g_ref[slot, e], preferred_element_type=F32)
                acc[...] += v * v

        if add is not None:
            k = exponent(extra[add])

            @pl.loop(0, rows // 16)
            def _(i):
                at = pl.ds(pl.multiple_of(i * 16, 16), 16)
                acc[at, :] += decode(extra[add][at, :], k)

        if coded:
            encode(acc, outs[j])


def blocks(jobs, a_refs, g, extra=()):
    n = len(jobs)
    most = max(j[2] for j in jobs)
    return pl.pallas_call(
        functools.partial(blocks_kernel, jobs, len(extra)),
        out_shape=[jax.ShapeDtypeStruct((j[2], 1024), BF if j[5] else F32) for j in jobs],
        in_specs=[ANY] * 11 + [VM] * (1 + len(extra)),
        out_specs=[VM] * n,
        scratch_shapes=[
            pltpu.VMEM((n, 4, 4, most, 128), BF),
            pltpu.VMEM((most, 1024), F32),
            pltpu.SemaphoreType.DMA((n, 4)),
        ],
        compiler_params=pltpu.CompilerParams(vmem_limit_bytes=VMEM_LIMIT),
        cost_estimate=pl.CostEstimate(flops=4 * n * 16 * 128 * 512 * 512, bytes_accessed=5 * n << 20, transcendentals=0),
        name="blocks_" + "_".join(f"{j[0] % 4}r{j[1]}" for j in jobs),
    )(*a_refs, g, *extra)


def final_kernel(part, own, p, *rest):
    o_ref, tmp, sem = rest[-3:]
    rows = ROWS[part]
    k = exponent(p)

    @pl.loop(0, rows // 16)
    def _(i):
        at = pl.ds(pl.multiple_of(i * 16, 16), 16)
        tmp[at, :] = own[at, :] + decode(p[at, :], k)
        to = pl.ds(pl.multiple_of(ROWS[0] * part + i * 16, 16), 16)
        pltpu.make_async_copy(tmp.at[at], o_ref.at[to], sem).start()

    pltpu.make_async_copy(tmp, tmp, sem).wait()


def final(part, own, payload, result=None):
    return pl.pallas_call(
        functools.partial(final_kernel, part),
        out_shape=jax.ShapeDtypeStruct((512, 1024), F32),
        in_specs=[VM] * 2 + ([] if result is None else [ANY]),
        out_specs=ANY,
        scratch_shapes=[pltpu.VMEM((ROWS[part], 1024), F32), pltpu.SemaphoreType.DMA],
        input_output_aliases={} if result is None else {2: 0},
        compiler_params=pltpu.CompilerParams(vmem_limit_bytes=VMEM_LIMIT),
        name=f"final{part}",
    )(own, payload, *(() if result is None else (result,)))


def send(v, axis, step):
    return lax.ppermute(v, axis, ring(2 if axis == "c" else 4, step))


def both_ways(v, axis):
    pairs = [(2 * i, 2 * ((i + 1) % 4)) for i in range(4)] + [(2 * i + 1, 2 * ((i + 3) % 4) + 1) for i in range(4)]
    return lax.ppermute(v, (axis, "c"), pairs)


def cross(v):
    return send(v, "c", 1)


def body(a, g):
    hold = lax.optimization_barrier
    gc = cross(g)
    p1 = prep(1, a)
    p0 = prep(0, a, p1)
    r1 = lax.ppermute(p1, ("z", "c"), round_pairs(1))
    r0 = lax.ppermute(p0, ("z", "c"), round_pairs(0))
    r1, gc = hold((r1, gc))
    r1c = cross(r1)
    r0, r1c = hold((r0, r1c))
    r0c = cross(r0)
    za = both_ways(jnp.stack([g[:2], gc[:2]]), "z")
    zb = both_ways(jnp.stack([g[2:], gc[2:]]), "z")
    m1 = both_ways(jnp.concatenate([r1, r1c]), "y")
    m0 = both_ways(jnp.concatenate([r0, r0c]), "y")
    m1, za = hold((m1, za))
    f1, fa, m1c = both_ways(m1[:4], "y"), both_ways(za[0], "z"), cross(m1)
    zac = cross(za[1])
    m0, zb, m1c, zac = hold((m0, zb, m1c, zac))
    f0, fb, m0c = both_ways(m0[:4], "y"), both_ways(zb[0], "z"), cross(m0)
    f1, zbh = hold((f1, zb[1]))
    zbc = cross(zbh)
    f0, f1, fa, fb, m0c, zac, zbc = hold((f0, f1, fa, fb, m0c, zac, zbc))
    fc = cross(jnp.concatenate([f0, f1]))
    gs = gather(g, za, zb, zac, zbc, fa, fb)
    a_refs = (r0, r1, r0c, r1c, m0, m1, m0c, m1c, f0, f1, fc)

    def run(jobs, extra=()):
        return blocks(jobs, a_refs, gs, extra)

    def job(d, part, add=None, coded=True):
        return (d, ROWS[0] * part, ROWS[part], None, add, coded, ALL)

    (early,) = blocks(((2, 0, 512, None, None, False, MINE),), (*a_refs[:10], r0), gs)
    (far0,) = run(((2, 0, ROWS[0], 0, None, True, THEIRS),), (early,))
    up0 = send(far0, "x", 1)
    (far1,) = run(((2, ROWS[0], ROWS[1], 0, None, True, THEIRS),), (early,))
    up1 = send(far1, "x", -1)
    (left0,) = run((job(-1, 0),))
    left0 = send(left0, "x", -1)
    (right1,) = run((job(1, 1),))
    right1 = send(right1, "x", 1)
    (right0,) = run((job(1, 0, 0),), (up0,))
    right0 = send(right0, "x", 1)
    (left1,) = run((job(-1, 1, 0),), (up1,))
    left1 = send(left1, "x", -1)
    (own1,) = run((job(0, 1, 0, False),), (right1,))
    (own0,) = run((job(0, 0, 0, False),), (left0,))
    return final(1, own1, left1, final(0, own0, right0))


def solution(mesh):
    fine = Mesh(mesh.devices.reshape(4, 4, 4, 2), ("x", "z", "y", "c"))
    spec = P(("x", "z"), None, ("y", "c"))
    return jax.shard_map(body, mesh=fine, in_specs=(spec, spec), out_specs=P(("x", "z"), ("y", "c")), check_vma=False)
```

```python
import functools

import jax
import jax.numpy as jnp
from jax import lax
from jax.experimental import pallas as pl
from jax.experimental.pallas import tpu as pltpu
from jax.sharding import Mesh, PartitionSpec as P

BF, F32 = jnp.bfloat16, jnp.float32
ANY = pl.BlockSpec(memory_space=pl.ANY)
VM = pl.BlockSpec(memory_space=pltpu.VMEM)
POWER = 12
TOP = 9.625
VMEM_LIMIT = 16 << 20


def ring(n, k):
    return [(i, (i + k) % n) for i in range(n)]


def code_of(u):
    return jnp.where(u == 0, 0, jnp.where(u == 1, 3, jnp.where(u == 2, 1, 2)))


def source_of(code):
    return jnp.where(code == 0, 0, jnp.where(code == 1, 2, jnp.where(code == 2, 3, 1)))


def round_pairs(k):
    pairs = []
    for z in range(4):
        for c in range(2):
            code = [0, 3, 1, 2][(z - 2 * c) % 4] ^ (2 * k)
            pairs.append((z * 2 + c, (2 * c + code // 2) * 2 + code % 2))
    return pairs


def prep_kernel(k, a_ref, *rest):
    o_ref, a_vm, sem = rest[-3:]
    z, c = lax.axis_index("z"), lax.axis_index("c")
    code = code_of(lax.rem(z - 2 * c + 4, 4)) ^ (2 * k)
    off = pl.multiple_of((code // 2) * 512, 512)
    copies = [pltpu.make_async_copy(a_ref.at[e, :, pl.ds(off, 512)], a_vm.at[e], sem.at[e]) for e in range(4)]
    for copy in copies:
        copy.start()
    for e in range(4):
        copies[e].wait()
        o_ref[e] = a_vm[e].T


def prep(k, a, *before):
    return pl.pallas_call(
        functools.partial(prep_kernel, k),
        out_shape=jax.ShapeDtypeStruct((4, 512, 128), BF),
        in_specs=[ANY] * (1 + len(before)),
        out_specs=VM,
        scratch_shapes=[pltpu.VMEM((4, 128, 512), BF), pltpu.SemaphoreType.DMA((4,))],
        compiler_params=pltpu.CompilerParams(vmem_limit_bytes=VMEM_LIMIT),
        name=f"prep{k}",
    )(a, *before)


def encode(acc, o_ref):
    rows, cols = acc.shape
    step = 16

    def largest(i, top):
        part = acc[pl.ds(pl.multiple_of(i * step, step), step), :].reshape(step // 8, 8, cols)
        return jnp.maximum(top, jnp.max(part, axis=0))

    top = lax.fori_loop(0, rows // step, largest, jnp.zeros((8, cols), F32))
    top = jnp.max(jnp.max(top, axis=0, keepdims=True), axis=1, keepdims=True)
    k = jnp.clip(jnp.floor(jnp.log2(jnp.maximum(top, 1e-36))), -100.0, 100.0)
    scale = jnp.exp2(TOP - k)

    def power(u):
        u2 = u * u
        u4 = u2 * u2
        return u4 * u4 * u4

    @pl.loop(0, rows // step)
    def _(i):
        at = pl.ds(pl.multiple_of(i * step, step), step)
        o_ref[at, :] = power(acc[at, :] * scale).astype(BF)

    lane, row = (lax.broadcasted_iota(jnp.int32, (16, 128), d) for d in (1, 0))
    shifted = jnp.floor((k + 128.0) * jnp.exp2(-lane.astype(F32)))
    odd = (shifted - 2.0 * jnp.floor(0.5 * shifted)) > 0.5
    t = power(acc[0:16, 0:128] * scale)
    coded = jnp.where(odd, -1.0, 1.0) * jnp.maximum(t, 1e-37)
    o_ref[0:16, 0:128] = jnp.where((row == 0) & (lane < 8), coded, t).astype(BF)


def exponent(p_ref):
    lane, row = (lax.broadcasted_iota(jnp.int32, (16, 128), d) for d in (1, 0))
    bit = (row == 0) & (lane < 8) & (p_ref[0:16, 0:128].astype(F32) < 0)
    value = jnp.where(bit, jnp.exp2(lane.astype(F32)), 0.0)
    return jnp.sum(jnp.sum(value, axis=0, keepdims=True), axis=1, keepdims=True) - 128.0


def decode(t, k):
    t = jnp.abs(t.astype(F32))
    root = jnp.exp2(jnp.log2(jnp.maximum(t, 1e-38)) * (1.0 / POWER))
    return jnp.where(t > 0, root, 0.0) * jnp.exp2(k - TOP)


def gather_kernel(g, za, zb, zac, zbc, fa, fb, o_ref, sem):
    c = lax.axis_index("c")
    near, far = jnp.where(c == 0, 3, 1), jnp.where(c == 0, 1, 3)
    copies = [
        pltpu.make_async_copy(g, o_ref.at[0], sem.at[0]),
        pltpu.make_async_copy(za.at[0], o_ref.at[near, 0:2], sem.at[1]),
        pltpu.make_async_copy(zb.at[0], o_ref.at[near, 2:4], sem.at[2]),
        pltpu.make_async_copy(zac, o_ref.at[far, 0:2], sem.at[3]),
        pltpu.make_async_copy(zbc, o_ref.at[far, 2:4], sem.at[6]),
        pltpu.make_async_copy(fa, o_ref.at[2, 0:2], sem.at[4]),
        pltpu.make_async_copy(fb, o_ref.at[2, 2:4], sem.at[5]),
    ]
    for copy in copies:
        copy.start()
    for copy in copies:
        copy.wait()


def gather(*pieces):
    return pl.pallas_call(
        gather_kernel,
        out_shape=jax.ShapeDtypeStruct((4, 4, 128, 1024), BF),
        in_specs=[ANY] * 7,
        out_specs=VM,
        scratch_shapes=[pltpu.SemaphoreType.DMA((7,))],
        compiler_params=pltpu.CompilerParams(vmem_limit_bytes=VMEM_LIMIT),
        name="gather",
    )(*pieces)


PIECES = {
    (0, None): ((0, 0), (1, 0), (2, 0), (3, 0)),
    (2, None): ((8, 0), (9, 0), (10, 0), (10, 4)),
    (3, 0): ((4, 0), (5, 0), (4, 4), (5, 4)),
    (3, 1): ((6, 4), (7, 4), (6, 0), (7, 0)),
    (1, 0): ((6, 4), (7, 4), (6, 0), (7, 0)),
    (1, 1): ((4, 0), (5, 0), (4, 4), (5, 4)),
}
ALL, MINE, THEIRS = (0, 1, 2, 3), (0, 1), (2, 3)
ROWS = (272, 240)


def blocks_kernel(jobs, n_extra, *refs):
    n = len(jobs)
    a_refs, g_ref = refs[:11], refs[11]
    extra = refs[12 : 12 + n_extra]
    outs = refs[12 + n_extra : 12 + n_extra + n]
    a_vm, acc_vm, sem = refs[12 + n_extra + n :]
    x, z, y, c = (lax.axis_index(name) for name in "xzyc")
    odd = lax.rem(z, 2)
    for j, (d, first_row, rows, _, _, _, pieces) in enumerate(jobs):
        r = lax.rem(x - y + d + 4, 4)
        for (value, on_core), places in PIECES.items():
            @pl.when(r == value if on_core is None else (r == value) & (c == on_core))
            def _():
                for piece in pieces:
                    ref, first = places[piece]
                    src = a_refs[ref].at[pl.ds(first, 4), pl.ds(first_row, rows), :]
                    pltpu.make_async_copy(src, a_vm.at[j, piece, :, 0:rows, :], sem.at[j, piece]).start()
    for j, (_, first_row, rows, begin, add, coded, pieces) in enumerate(jobs):
        acc = acc_vm.at[0:rows] if coded else outs[j]
        if begin is None:
            acc[...] = jnp.zeros_like(acc)
        else:
            acc[...] = extra[begin][first_row : first_row + rows, :]

        @pl.loop(pieces[0], pieces[-1] + 1)
        def _(piece):
            core = jnp.where(piece < 2, c, 1 - c)
            slot = lax.rem(source_of((2 * odd + core) ^ (2 * lax.rem(piece, 2))) - odd + 4, 4)
            held = a_vm.at[j, piece, :, 0:rows, :]
            pltpu.make_async_copy(held, held, sem.at[j, piece]).wait()
            for e in range(4):
                v = jnp.dot(a_vm[j, piece, e, 0:rows, :], g_ref[slot, e], preferred_element_type=F32)
                acc[...] += v * v

        if add is not None:
            k = exponent(extra[add])

            @pl.loop(0, rows // 16)
            def _(i):
                at = pl.ds(pl.multiple_of(i * 16, 16), 16)
                acc[at, :] += decode(extra[add][at, :], k)

        if coded:
            encode(acc, outs[j])


def blocks(jobs, a_refs, g, extra=()):
    n = len(jobs)
    most = max(j[2] for j in jobs)
    return pl.pallas_call(
        functools.partial(blocks_kernel, jobs, len(extra)),
        out_shape=[jax.ShapeDtypeStruct((j[2], 1024), BF if j[5] else F32) for j in jobs],
        in_specs=[ANY] * 11 + [VM] * (1 + len(extra)),
        out_specs=[VM] * n,
        scratch_shapes=[
            pltpu.VMEM((n, 4, 4, most, 128), BF),
            pltpu.VMEM((most, 1024), F32),
            pltpu.SemaphoreType.DMA((n, 4)),
        ],
        compiler_params=pltpu.CompilerParams(vmem_limit_bytes=VMEM_LIMIT),
        cost_estimate=pl.CostEstimate(flops=4 * n * 16 * 128 * 512 * 512, bytes_accessed=5 * n << 20, transcendentals=0),
        name="blocks_" + "_".join(f"{j[0] % 4}r{j[1]}" for j in jobs),
    )(*a_refs, g, *extra)


def final_kernel(part, own, p, *rest):
    o_ref, tmp, sem = rest[-3:]
    rows = ROWS[part]
    k = exponent(p)

    @pl.loop(0, rows // 16)
    def _(i):
        at = pl.ds(pl.multiple_of(i * 16, 16), 16)
        tmp[at, :] = own[at, :] + decode(p[at, :], k)
        to = pl.ds(pl.multiple_of(ROWS[0] * part + i * 16, 16), 16)
        pltpu.make_async_copy(tmp.at[at], o_ref.at[to], sem).start()

    pltpu.make_async_copy(tmp, tmp, sem).wait()


def final(part, own, payload, result=None):
    return pl.pallas_call(
        functools.partial(final_kernel, part),
        out_shape=jax.ShapeDtypeStruct((512, 1024), F32),
        in_specs=[VM] * 2 + ([] if result is None else [ANY]),
        out_specs=ANY,
        scratch_shapes=[pltpu.VMEM((ROWS[part], 1024), F32), pltpu.SemaphoreType.DMA],
        input_output_aliases={} if result is None else {2: 0},
        compiler_params=pltpu.CompilerParams(vmem_limit_bytes=VMEM_LIMIT),
        name=f"final{part}",
    )(own, payload, *(() if result is None else (result,)))


def send(v, axis, step):
    return lax.ppermute(v, axis, ring(2 if axis == "c" else 4, step))


def both_ways(v, axis):
    pairs = [(2 * i, 2 * ((i + 1) % 4)) for i in range(4)] + [(2 * i + 1, 2 * ((i + 3) % 4) + 1) for i in range(4)]
    return lax.ppermute(v, (axis, "c"), pairs)


def cross(v):
    return send(v, "c", 1)


def body(a, g):
    hold = lax.optimization_barrier
    gc = cross(g)
    p1 = prep(1, a)
    p0 = prep(0, a, p1)
    r1 = lax.ppermute(p1, ("z", "c"), round_pairs(1))
    r0 = lax.ppermute(p0, ("z", "c"), round_pairs(0))
    r1, gc = hold((r1, gc))
    r1c = cross(r1)
    r0, r1c = hold((r0, r1c))
    r0c = cross(r0)
    za = both_ways(jnp.stack([g[:2], gc[:2]]), "z")
    zb = both_ways(jnp.stack([g[2:], gc[2:]]), "z")
    m1 = both_ways(jnp.concatenate([r1, r1c]), "y")
    m0 = both_ways(jnp.concatenate([r0, r0c]), "y")
    m1, za = hold((m1, za))
    f1, fa, m1c = both_ways(m1[:4], "y"), both_ways(za[0], "z"), cross(m1)
    m0, zb, m1c, zah = hold((m0, zb, m1c, za[1]))
    f0, fb, m0c = both_ways(m0[:4], "y"), both_ways(zb[0], "z"), cross(m0)
    zac, zbc = cross(zah), cross(zb[1])
    f0, f1, fa, fb, m0c, zac, zbc = hold((f0, f1, fa, fb, m0c, zac, zbc))
    fc = cross(jnp.concatenate([f0, f1]))
    gs = gather(g, za, zb, zac, zbc, fa, fb)
    a_refs = (r0, r1, r0c, r1c, m0, m1, m0c, m1c, f0, f1, fc)

    def run(jobs, extra=()):
        return blocks(jobs, a_refs, gs, extra)

    def job(d, part, add=None, coded=True):
        return (d, ROWS[0] * part, ROWS[part], None, add, coded, ALL)

    (early,) = blocks(((2, 0, 512, None, None, False, MINE),), (*a_refs[:10], r0), gs)
    (far0,) = run(((2, 0, ROWS[0], 0, None, True, THEIRS),), (early,))
    up0 = send(far0, "x", 1)
    (far1,) = run(((2, ROWS[0], ROWS[1], 0, None, True, THEIRS),), (early,))
    up1 = send(far1, "x", -1)
    (left0,) = run((job(-1, 0),))
    left0 = send(left0, "x", -1)
    (right1,) = run((job(1, 1),))
    right1 = send(right1, "x", 1)
    (right0,) = run((job(1, 0, 0),), (up0,))
    right0 = send(right0, "x", 1)
    (left1,) = run((job(-1, 1, 0),), (up1,))
    left1 = send(left1, "x", -1)
    (own1,) = run((job(0, 1, 0, False),), (right1,))
    (own0,) = run((job(0, 0, 0, False),), (left0,))
    return final(1, own1, left1, final(0, own0, right0))


def solution(mesh):
    fine = Mesh(mesh.devices.reshape(4, 4, 4, 2), ("x", "z", "y", "c"))
    spec = P(("x", "z"), None, ("y", "c"))
    return jax.shard_map(body, mesh=fine, in_specs=(spec, spec), out_specs=P(("x", "z"), ("y", "c")), check_vma=False)
```

```python
import functools

import jax
import jax.numpy as jnp
from jax import lax
from jax.experimental import pallas as pl
from jax.experimental.pallas import tpu as pltpu
from jax.sharding import Mesh, PartitionSpec as P

BF, F32 = jnp.bfloat16, jnp.float32
ANY = pl.BlockSpec(memory_space=pl.ANY)
VM = pl.BlockSpec(memory_space=pltpu.VMEM)
POWER = 12
TOP = 9.625
VMEM_LIMIT = 16 << 20


def ring(n, k):
    return [(i, (i + k) % n) for i in range(n)]


def code_of(u):
    return jnp.where(u == 0, 0, jnp.where(u == 1, 3, jnp.where(u == 2, 1, 2)))


def source_of(code):
    return jnp.where(code == 0, 0, jnp.where(code == 1, 2, jnp.where(code == 2, 3, 1)))


def round_pairs(k):
    pairs = []
    for z in range(4):
        for c in range(2):
            code = [0, 3, 1, 2][(z - 2 * c) % 4] ^ (2 * k)
            pairs.append((z * 2 + c, (2 * c + code // 2) * 2 + code % 2))
    return pairs


def prep_kernel(k, a_ref, *rest):
    o_ref, a_vm, sem = rest[-3:]
    z, c = lax.axis_index("z"), lax.axis_index("c")
    code = code_of(lax.rem(z - 2 * c + 4, 4)) ^ (2 * k)
    off = pl.multiple_of((code // 2) * 512, 512)
    copies = [pltpu.make_async_copy(a_ref.at[e, :, pl.ds(off, 512)], a_vm.at[e], sem.at[e]) for e in range(4)]
    for copy in copies:
        copy.start()
    for e in range(4):
        copies[e].wait()
        o_ref[e] = a_vm[e].T


def prep(k, a, *before):
    return pl.pallas_call(
        functools.partial(prep_kernel, k),
        out_shape=jax.ShapeDtypeStruct((4, 512, 128), BF),
        in_specs=[ANY] * (1 + len(before)),
        out_specs=VM,
        scratch_shapes=[pltpu.VMEM((4, 128, 512), BF), pltpu.SemaphoreType.DMA((4,))],
        compiler_params=pltpu.CompilerParams(vmem_limit_bytes=VMEM_LIMIT),
        name=f"prep{k}",
    )(a, *before)


def encode(acc, o_ref):
    rows, cols = acc.shape
    step = 16

    def largest(i, top):
        part = acc[pl.ds(pl.multiple_of(i * step, step), step), :].reshape(step // 8, 8, cols)
        return jnp.maximum(top, jnp.max(part, axis=0))

    top = lax.fori_loop(0, rows // step, largest, jnp.zeros((8, cols), F32))
    top = jnp.max(jnp.max(top, axis=0, keepdims=True), axis=1, keepdims=True)
    k = jnp.clip(jnp.floor(jnp.log2(jnp.maximum(top, 1e-36))), -100.0, 100.0)
    scale = jnp.exp2(TOP - k)

    def power(u):
        u2 = u * u
        u4 = u2 * u2
        return u4 * u4 * u4

    @pl.loop(0, rows // step)
    def _(i):
        at = pl.ds(pl.multiple_of(i * step, step), step)
        o_ref[at, :] = power(acc[at, :] * scale).astype(BF)

    lane, row = (lax.broadcasted_iota(jnp.int32, (16, 128), d) for d in (1, 0))
    shifted = jnp.floor((k + 128.0) * jnp.exp2(-lane.astype(F32)))
    odd = (shifted - 2.0 * jnp.floor(0.5 * shifted)) > 0.5
    t = power(acc[0:16, 0:128] * scale)
    coded = jnp.where(odd, -1.0, 1.0) * jnp.maximum(t, 1e-37)
    o_ref[0:16, 0:128] = jnp.where((row == 0) & (lane < 8), coded, t).astype(BF)


def exponent(p_ref):
    lane, row = (lax.broadcasted_iota(jnp.int32, (16, 128), d) for d in (1, 0))
    bit = (row == 0) & (lane < 8) & (p_ref[0:16, 0:128].astype(F32) < 0)
    value = jnp.where(bit, jnp.exp2(lane.astype(F32)), 0.0)
    return jnp.sum(jnp.sum(value, axis=0, keepdims=True), axis=1, keepdims=True) - 128.0


def decode(t, k):
    t = jnp.abs(t.astype(F32))
    root = jnp.exp2(jnp.log2(jnp.maximum(t, 1e-38)) * (1.0 / POWER))
    return jnp.where(t > 0, root, 0.0) * jnp.exp2(k - TOP)


def gather_kernel(g, za, zb, zac, zbc, fa, fb, o_ref, sem):
    c = lax.axis_index("c")
    near, far = jnp.where(c == 0, 3, 1), jnp.where(c == 0, 1, 3)
    copies = [
        pltpu.make_async_copy(g, o_ref.at[0], sem.at[0]),
        pltpu.make_async_copy(za.at[0], o_ref.at[near, 0:2], sem.at[1]),
        pltpu.make_async_copy(zb.at[0], o_ref.at[near, 2:4], sem.at[2]),
        pltpu.make_async_copy(zac, o_ref.at[far, 0:2], sem.at[3]),
        pltpu.make_async_copy(zbc, o_ref.at[far, 2:4], sem.at[6]),
        pltpu.make_async_copy(fa, o_ref.at[2, 0:2], sem.at[4]),
        pltpu.make_async_copy(fb, o_ref.at[2, 2:4], sem.at[5]),
    ]
    for copy in copies:
        copy.start()
    for copy in copies:
        copy.wait()


def gather(*pieces):
    return pl.pallas_call(
        gather_kernel,
        out_shape=jax.ShapeDtypeStruct((4, 4, 128, 1024), BF),
        in_specs=[ANY] * 7,
        out_specs=VM,
        scratch_shapes=[pltpu.SemaphoreType.DMA((7,))],
        compiler_params=pltpu.CompilerParams(vmem_limit_bytes=VMEM_LIMIT),
        name="gather",
    )(*pieces)


PIECES = {
    (0, None): ((0, 0), (1, 0), (2, 0), (3, 0)),
    (2, None): ((8, 0), (9, 0), (10, 0), (10, 4)),
    (3, 0): ((4, 0), (5, 0), (4, 4), (5, 4)),
    (3, 1): ((6, 4), (7, 4), (6, 0), (7, 0)),
    (1, 0): ((6, 4), (7, 4), (6, 0), (7, 0)),
    (1, 1): ((4, 0), (5, 0), (4, 4), (5, 4)),
}
ALL, MINE, THEIRS = (0, 1, 2, 3), (0, 1), (2, 3)
ROWS = (272, 240)


def blocks_kernel(jobs, n_extra, *refs):
    n = len(jobs)
    a_refs, g_ref = refs[:11], refs[11]
    extra = refs[12 : 12 + n_extra]
    outs = refs[12 + n_extra : 12 + n_extra + n]
    a_vm, acc_vm, sem = refs[12 + n_extra + n :]
    x, z, y, c = (lax.axis_index(name) for name in "xzyc")
    odd = lax.rem(z, 2)
    for j, (d, first_row, rows, _, _, _, pieces) in enumerate(jobs):
        r = lax.rem(x - y + d + 4, 4)
        for (value, on_core), places in PIECES.items():
            @pl.when(r == value if on_core is None else (r == value) & (c == on_core))
            def _():
                for piece in pieces:
                    ref, first = places[piece]
                    src = a_refs[ref].at[pl.ds(first, 4), pl.ds(first_row, rows), :]
                    pltpu.make_async_copy(src, a_vm.at[j, piece, :, 0:rows, :], sem.at[j, piece]).start()
    for j, (_, first_row, rows, begin, add, coded, pieces) in enumerate(jobs):
        acc = acc_vm.at[0:rows] if coded else outs[j]
        if begin is None:
            acc[...] = jnp.zeros_like(acc)
        else:
            acc[...] = extra[begin][first_row : first_row + rows, :]

        @pl.loop(pieces[0], pieces[-1] + 1)
        def _(piece):
            core = jnp.where(piece < 2, c, 1 - c)
            slot = lax.rem(source_of((2 * odd + core) ^ (2 * lax.rem(piece, 2))) - odd + 4, 4)
            held = a_vm.at[j, piece, :, 0:rows, :]
            pltpu.make_async_copy(held, held, sem.at[j, piece]).wait()
            for e in range(4):
                v = jnp.dot(a_vm[j, piece, e, 0:rows, :], g_ref[slot, e], preferred_element_type=F32)
                acc[...] += v * v

        if add is not None:
            k = exponent(extra[add])

            @pl.loop(0, rows // 16)
            def _(i):
                at = pl.ds(pl.multiple_of(i * 16, 16), 16)
                acc[at, :] += decode(extra[add][at, :], k)

        if coded:
            encode(acc, outs[j])


def blocks(jobs, a_refs, g, extra=()):
    n = len(jobs)
    most = max(j[2] for j in jobs)
    return pl.pallas_call(
        functools.partial(blocks_kernel, jobs, len(extra)),
        out_shape=[jax.ShapeDtypeStruct((j[2], 1024), BF if j[5] else F32) for j in jobs],
        in_specs=[ANY] * 11 + [VM] * (1 + len(extra)),
        out_specs=[VM] * n,
        scratch_shapes=[
            pltpu.VMEM((n, 4, 4, most, 128), BF),
            pltpu.VMEM((most, 1024), F32),
            pltpu.SemaphoreType.DMA((n, 4)),
        ],
        compiler_params=pltpu.CompilerParams(vmem_limit_bytes=VMEM_LIMIT),
        cost_estimate=pl.CostEstimate(flops=4 * n * 16 * 128 * 512 * 512, bytes_accessed=5 * n << 20, transcendentals=0),
        name="blocks_" + "_".join(f"{j[0] % 4}r{j[1]}" for j in jobs),
    )(*a_refs, g, *extra)


def final_kernel(part, own, p, *rest):
    o_ref, tmp, sem = rest[-3:]
    rows = ROWS[part]
    k = exponent(p)

    @pl.loop(0, rows // 16)
    def _(i):
        at = pl.ds(pl.multiple_of(i * 16, 16), 16)
        tmp[at, :] = own[at, :] + decode(p[at, :], k)
        to = pl.ds(pl.multiple_of(ROWS[0] * part + i * 16, 16), 16)
        pltpu.make_async_copy(tmp.at[at], o_ref.at[to], sem).start()

    pltpu.make_async_copy(tmp, tmp, sem).wait()


def final(part, own, payload, result=None):
    return pl.pallas_call(
        functools.partial(final_kernel, part),
        out_shape=jax.ShapeDtypeStruct((512, 1024), F32),
        in_specs=[VM] * 2 + ([] if result is None else [ANY]),
        out_specs=ANY,
        scratch_shapes=[pltpu.VMEM((ROWS[part], 1024), F32), pltpu.SemaphoreType.DMA],
        input_output_aliases={} if result is None else {2: 0},
        compiler_params=pltpu.CompilerParams(vmem_limit_bytes=VMEM_LIMIT),
        name=f"final{part}",
    )(own, payload, *(() if result is None else (result,)))


def send(v, axis, step):
    return lax.ppermute(v, axis, ring(2 if axis == "c" else 4, step))


def both_ways(v, axis):
    pairs = [(2 * i, 2 * ((i + 1) % 4)) for i in range(4)] + [(2 * i + 1, 2 * ((i + 3) % 4) + 1) for i in range(4)]
    return lax.ppermute(v, (axis, "c"), pairs)


def cross(v):
    return send(v, "c", 1)


def body(a, g):
    hold = lax.optimization_barrier
    gc = cross(g)
    p1 = prep(1, a)
    p0 = prep(0, a, p1)
    r1 = lax.ppermute(p1, ("z", "c"), round_pairs(1))
    r0 = lax.ppermute(p0, ("z", "c"), round_pairs(0))
    r1, gc = hold((r1, gc))
    r1c = cross(r1)
    r0, r1c = hold((r0, r1c))
    r0c = cross(r0)
    za = both_ways(jnp.stack([g[:2], gc[:2]]), "z")
    zb = both_ways(jnp.stack([g[2:], gc[2:]]), "z")
    m1 = both_ways(jnp.concatenate([r1, r1c]), "y")
    m0 = both_ways(jnp.concatenate([r0, r0c]), "y")
    m1, za = hold((m1, za))
    f1, fa, m1c = both_ways(m1[:4], "y"), both_ways(za[0], "z"), cross(m1)
    m0, zb, m1c, zah = hold((m0, zb, m1c, za[1]))
    f0, fb, m0c = both_ways(m0[:4], "y"), both_ways(zb[0], "z"), cross(m0)
    zac, zbc = cross(zah), cross(zb[1])
    f0, f1, fa, fb, m0c = hold((f0, f1, fa, fb, m0c))
    fc = cross(jnp.concatenate([f0, f1]))
    gs = gather(g, za, zb, zac, zbc, fa, fb)
    a_refs = (r0, r1, r0c, r1c, m0, m1, m0c, m1c, f0, f1, fc)

    def run(jobs, extra=()):
        return blocks(jobs, a_refs, gs, extra)

    def job(d, part, add=None, coded=True):
        return (d, ROWS[0] * part, ROWS[part], None, add, coded, ALL)

    (early,) = blocks(((2, 0, 512, None, None, False, MINE),), (*a_refs[:10], r0), gs)
    (far0,) = run(((2, 0, ROWS[0], 0, None, True, THEIRS),), (early,))
    up0 = send(far0, "x", 1)
    (far1,) = run(((2, ROWS[0], ROWS[1], 0, None, True, THEIRS),), (early,))
    up1 = send(far1, "x", -1)
    (left0,) = run((job(-1, 0),))
    left0 = send(left0, "x", -1)
    (right1,) = run((job(1, 1),))
    right1 = send(right1, "x", 1)
    (right0,) = run((job(1, 0, 0),), (up0,))
    right0 = send(right0, "x", 1)
    (left1,) = run((job(-1, 1, 0),), (up1,))
    left1 = send(left1, "x", -1)
    (own1,) = run((job(0, 1, 0, False),), (right1,))
    (own0,) = run((job(0, 0, 0, False),), (left0,))
    return final(1, own1, left1, final(0, own0, right0))


def solution(mesh):
    fine = Mesh(mesh.devices.reshape(4, 4, 4, 2), ("x", "z", "y", "c"))
    spec = P(("x", "z"), None, ("y", "c"))
    return jax.shard_map(body, mesh=fine, in_specs=(spec, spec), out_specs=P(("x", "z"), ("y", "c")), check_vma=False)
```
